256 devices in a mesh: prompt: 16 (over x, z_hi), seq: 16 (over z_lo, y, core).
Axes of the slice: x: 4, y: 4, z: 8 (z_hi: 4, z_lo: 2; z = z_hi * 2 + z_lo), core: 2. Of those that a mesh axis runs over, the one named last changes fastest.
Arguments:
- queries: bfloat16 [16, 8192, 1024], P('prompt', 'seq'), may hold values from -5 to 5
- resp_kv: bfloat16 [16, 8192, 256], P('prompt', 'seq'), may hold values from -16 to 16
- prefix_kv: bfloat16 [16, 768, 256], P('prompt', 'seq'), may hold values from -16 to 16
- lengths: int32 [16, 16], P('prompt'), may hold values from 256 to 512, as said below
- upstream: bfloat16 [16, 8192, 1024], P('prompt', 'seq'), may hold values from -6 to 6
Outputs:
- attended: bfloat16 [16, 8192, 1024], P('prompt', 'seq')
- grad_queries: bfloat16 [16, 8192, 1024], P('prompt', 'seq')
- grad_resp_kv: float32 [16, 8192, 256], P('prompt', 'seq')
- grad_prefix_kv: float32 [16, 768, 256], P('prompt', 'seq')
The draws below stay inside these ranges and needn't reach their ends.
Inputs may be any that keep to these rules, and one draw needn't show every extreme that they name: `lengths`: each prompt's 16 responses fill its slots in order from slot 0; one response of every prompt has exactly 512 tokens.
All inputs are finite; a program needn't handle non-finite values.
Results may differ from the reference program's by a relative error of at most 0.011.
Values may be sent and summed in bfloat16 or wider, within the bound.
No kernel may reach another device: no remote copies, remote signals or barrier semaphores. Data moves between devices by JAX's collectives and lax.ppermute only.
A program may use at most 192 MiB of HBM per device.

```python
import jax
import jax.numpy as jnp
from jax import lax

HQ = 8
DH = 128
LMAX = 512
PROMPTS = 16
NRESP = 16
SLOTS = 8192
PREFIX = 768
N_SEQ = 16


def draw_queries(key, part):
    key = jax.random.fold_in(key, 11)
    base = jnp.clip(jax.random.normal(key, (PROMPTS, SLOTS, HQ * DH), jnp.float32), -4.0, 4.0)
    return base.astype(jnp.bfloat16)


def draw_prefix_kv(key, part):
    key = jax.random.fold_in(key, 12)
    key_keys, key_values = jax.random.split(key)
    key_part = jnp.clip(jax.random.normal(key_keys, (PROMPTS, PREFIX, DH), jnp.float32), -4.0, 4.0)
    value_part = 4.0 * jnp.clip(jax.random.normal(key_values, (PROMPTS, PREFIX, DH), jnp.float32), -4.0, 4.0)
    return jnp.concatenate([key_part, value_part], axis=-1).astype(jnp.bfloat16)


def draw_resp_kv(key, part):
    key = jax.random.fold_in(key, 13)
    key_keys, key_values = jax.random.split(key)
    key_part = jnp.clip(jax.random.normal(key_keys, (PROMPTS, SLOTS, DH), jnp.float32), -4.0, 4.0)
    value_part = 4.0 * jnp.clip(jax.random.normal(key_values, (PROMPTS, SLOTS, DH), jnp.float32), -4.0, 4.0)
    return jnp.concatenate([key_part, value_part], axis=-1).astype(jnp.bfloat16)


def draw_lengths(key, part):
    key = jax.random.fold_in(key, 14)
    key_base, key_place = jax.random.split(key)
    base = jax.random.randint(key_base, (PROMPTS, NRESP), LMAX // 2, LMAX + 1)
    place = jax.random.randint(key_place, (PROMPTS,), 0, NRESP)
    chosen = jnp.arange(NRESP, dtype=jnp.int32)[None, :] == place[:, None]
    return jnp.where(chosen, LMAX, base).astype(jnp.int32)


def block_levels(key, shape, cuts, low, top_value):
    def one(dim, shards_of):
        heights = jax.random.uniform(jax.random.fold_in(jax.random.fold_in(key, 6), dim), (shards_of,), jnp.float32, low / len(cuts), top_value / len(cuts))
        return jnp.repeat(jnp.exp(heights), shape[dim] // shards_of).reshape((-1,) + (1,) * (len(shape) - dim - 1))

    factor_of = one(*cuts[0])
    for cut in cuts[1:]:
        factor_of = factor_of * one(*cut)
    return factor_of


def scatter_about(rng, dims, width, bound, cuts=(), kind=jnp.bfloat16):
    values = width * jax.random.normal(rng, dims, jnp.float32)
    if cuts:
        values = values * block_levels(rng, dims, cuts, -0.22, 0.18)
    return jnp.clip(values, -bound, bound).astype(kind)


def setup_inputs(seed: int = 0) -> dict:
    key_list = jax.random.split(jax.random.key(seed), 6)
    return {
        "queries": draw_queries(jax.random.fold_in(key_list[5], 71), 0),
        "resp_kv": draw_resp_kv(jax.random.fold_in(key_list[5], 71), 0),
        "prefix_kv": draw_prefix_kv(jax.random.fold_in(key_list[5], 71), 0),
        "lengths": draw_lengths(jax.random.fold_in(key_list[5], 71), 0),
        "upstream": scatter_about(key_list[4], (PROMPTS, SLOTS, HQ * DH), 1.0, 6.0, ((0, 16), (1, 16))),
    }


def rounded(values):
    return lax.optimization_barrier(values.astype(jnp.bfloat16)).astype(jnp.float32)


def slot_segments(resp_ends, slot_ids):
    counted = jnp.sum((slot_ids[:, None] >= resp_ends[None, :]).astype(jnp.int32), axis=1)
    return jnp.where(slot_ids < 0, -1, counted).astype(jnp.int32)


def shard_terms(query_rows, key_vals, visible, live_rows, upstream_rows, factor):
    head_dim = query_rows.shape[-1]
    score_scale = head_dim ** -0.5
    key_part = key_vals[:, :head_dim].astype(jnp.float32)
    value_part = key_vals[:, head_dim:].astype(jnp.float32)
    query_f = query_rows.astype(jnp.float32)
    scores = jnp.einsum('rhd,kd->rhk', query_f, key_part) * score_scale
    scores = jnp.where(visible[:, None, :], scores, -jnp.inf)
    row_max = jnp.max(scores, axis=-1, keepdims=True)
    weights = jnp.exp(scores - row_max)
    row_total = jnp.sum(weights, axis=-1, keepdims=True)
    mixed = jnp.einsum('rhk,kd->rhd', rounded(weights), value_part) / row_total
    attended = (mixed * live_rows[:, None, None]).astype(jnp.bfloat16)
    log_total = row_max + jnp.log(row_total)
    grad_out = rounded(upstream_rows.astype(jnp.float32) * factor * live_rows[:, None, None])
    delta = jnp.sum(grad_out * attended.astype(jnp.float32), axis=-1, keepdims=True)
    probs = jnp.exp(scores - log_total)
    dprobs = jnp.einsum('rhd,kd->rhk', grad_out, value_part)
    dscores = rounded(probs * (dprobs - delta))
    probs_low = rounded(probs)
    grad_query = (jnp.einsum('rhk,kd->rhd', dscores, key_part) * score_scale).astype(jnp.bfloat16)
    key_grads = jnp.einsum('rhk,rhd->kd', dscores, query_f) * score_scale
    value_grads = jnp.einsum('rhk,rhd->kd', probs_low, grad_out)
    return attended, grad_query, jnp.concatenate([key_grads, value_grads], axis=1)


def reference(queries, resp_kv, prefix_kv, lengths, upstream):
    factor = jnp.float32(PROMPTS * SLOTS) / jnp.sum(lengths).astype(jnp.float32)

    def one_prompt(items):
        query_all, kv_all, prefix_all, length_row, upstream_all = items
        resp_ends = jnp.cumsum(length_row).astype(jnp.int32)
        query_four = query_all.reshape(N_SEQ, LMAX, HQ, DH)
        upstream_four = upstream_all.reshape(N_SEQ, LMAX, HQ, DH)
        kv_three = kv_all.reshape(N_SEQ, LMAX, 2 * DH)
        earlier = jnp.concatenate([jnp.zeros((1, LMAX, 2 * DH), kv_all.dtype), kv_three[:-1]], axis=0)

        def step(carry, inputs):
            query_rows, upstream_rows, own_kv, prev_kv, shard_index = inputs
            positions = shard_index * LMAX + jnp.arange(LMAX, dtype=jnp.int32)
            own_seg = slot_segments(resp_ends, positions)
            prev_seg = slot_segments(resp_ends, positions - LMAX)
            live_rows = (own_seg < NRESP).astype(jnp.float32)
            key_slots = jnp.concatenate([positions - LMAX, positions])
            key_segs = jnp.concatenate([prev_seg, own_seg])
            same_resp = (key_segs[None, :] == own_seg[:, None]) & (key_slots[None, :] <= positions[:, None])
            visible = jnp.concatenate([jnp.ones((LMAX, PREFIX), jnp.bool_), same_resp], axis=1)
            key_vals = jnp.concatenate([prefix_all, prev_kv, own_kv], axis=0)
            attended, grad_query, kv_grads = shard_terms(query_rows, key_vals, visible, live_rows, upstream_rows, factor)
            carry = carry + kv_grads[:PREFIX]
            return carry, (attended, grad_query, kv_grads[PREFIX:PREFIX + LMAX], kv_grads[PREFIX + LMAX:])

        start = jnp.zeros((PREFIX, 2 * DH), jnp.float32)
        prefix_grads, stacked = lax.scan(step, start, (query_four, upstream_four, kv_three, earlier, jnp.arange(N_SEQ, dtype=jnp.int32)))
        attended, grad_query, prev_grads, own_grads = stacked
        later = jnp.concatenate([prev_grads[1:], jnp.zeros((1, LMAX, 2 * DH), jnp.float32)], axis=0)
        resp_grads = own_grads + later
        return (attended.reshape(SLOTS, HQ * DH), grad_query.reshape(SLOTS, HQ * DH), resp_grads.reshape(SLOTS, 2 * DH), prefix_grads)

    attended, grad_queries, grad_resp_kv, grad_prefix_kv = lax.map(one_prompt, (queries, resp_kv, prefix_kv, lengths, upstream))
    return (attended, grad_queries, grad_resp_kv, grad_prefix_kv)
```

```python
import math

import jax
import jax.numpy as jnp
from jax import lax
from jax.experimental import pallas as pl
from jax.experimental.pallas import tpu as pltpu
from jax.sharding import PartitionSpec as P
F32=jnp.float32; BF=jnp.bfloat16
NT=(((1,),(1,)),((),()))
NN=(((1,),(0,)),((),()))
def dot(a,b,dims=NN):
    return lax.dot_general(a,b,dims,preferred_element_type=F32)

def kernel(len_ref, shard_ref, q_ref, up_ref, kvp_ref, kvprev_ref, kvown_ref,
           o_ref, gq_ref, gp_ref, gw_ref,
           k_s, v_s, kt_s, vt_s, bias_s, s_s, w_s, ds_s, gk_s, gv_s):
    dh=128; rows=q_ref.shape[0]; npre=kvp_ref.shape[0]; heads=q_ref.shape[1]//dh
    rb=128; win=rows+rb; nk=npre+win; nresp=len_ref.shape[1]
    scale=dh**-0.5
    c2=scale*math.log2(math.e)
    tot=npre+2*rows
    k_s[0:npre]=kvp_ref[:,0:dh]; v_s[0:npre]=kvp_ref[:,dh:]
    k_s[npre:npre+rows]=kvprev_ref[:,0:dh]; v_s[npre:npre+rows]=kvprev_ref[:,dh:]
    k_s[npre+rows:]=kvown_ref[:,0:dh]; v_s[npre+rows:]=kvown_ref[:,dh:]
    kt_s[...]=k_s[...].T
    vt_s[...]=v_s[...].T
    gk_s[...]=jnp.zeros_like(gk_s); gv_s[...]=jnp.zeros_like(gv_s)
    shard=shard_ref[0]
    def block(i,_):
        r0=pl.multiple_of(i*rb,rb)
        w0=pl.multiple_of(npre+i*rb,rb)
        pos=shard*rows+r0+lax.broadcasted_iota(jnp.int32,(1,rb),1)
        lo=jnp.zeros((1,rb),jnp.int32); end=jnp.int32(0)
        for r in range(nresp):
            end=end+len_ref[0,r]
            lo=jnp.where(pos>=end,end,lo)
        live_row=(pos<end)
        u=(shard-1)*rows+r0+lax.broadcasted_iota(jnp.int32,(win,rb),0)
        bias_s[...]=jnp.where((u>=lo)&(u<=pos),0.0,-jnp.inf).astype(F32)
        def pair(p,_):
            c0=pl.multiple_of(p*2*dh,2*dh)
            q2=q_ref[pl.ds(r0,rb),pl.ds(c0,2*dh)]
            q=jnp.concatenate([q2[:,:dh],q2[:,dh:]],axis=0)
            up2=up_ref[pl.ds(r0,rb),pl.ds(c0,2*dh)]
            up=jnp.concatenate([up2[:,:dh],up2[:,dh:]],axis=0)
            s_s[0:npre]=dot(k_s[0:npre],q,NT)
            s_s[npre:]=dot(k_s[pl.ds(w0,win)],q,NT)
            ch=128
            m=jnp.full((8,2*rb),-jnp.inf,F32)
            for j in range(nk//ch):
                s=s_s[j*ch:(j+1)*ch]*c2
                if j*ch>=npre:
                    b=bias_s[j*ch-npre:(j+1)*ch-npre]
                    s=s+jnp.concatenate([b,b],axis=1)
                s_s[j*ch:(j+1)*ch]=s
                m=jnp.maximum(m,jnp.max(s.reshape(ch//8,8,2*rb),axis=0))
            m=jnp.max(m,axis=0,keepdims=True)
            l=jnp.zeros((8,2*rb),F32)
            for j in range(nk//ch):
                w=jnp.exp2(s_s[j*ch:(j+1)*ch]-m)
                l=l+jnp.sum(w.reshape(ch//8,8,2*rb),axis=0)
                w_s[j*ch:(j+1)*ch]=w.astype(BF)
            l=jnp.sum(l,axis=0,keepdims=True)
            live2=jnp.concatenate([live_row,live_row],axis=1)
            inv=jnp.where(live2,1.0/l,0.0)
            ot=dot(vt_s[:,0:npre],w_s[0:npre])+dot(vt_s[:,pl.ds(w0,win)],w_s[npre:])
            ot=ot*inv
            o=ot.T
            ob=o.astype(BF)
            invc=jnp.broadcast_to(inv,(dh,2*rb)).T
            dof=up.astype(F32)*invc
            dob=dof.astype(BF)
            o_ref[pl.ds(r0,rb),pl.ds(c0,2*dh)]=jnp.concatenate([ob[:rb],ob[rb:]],axis=1)
            prod=(dob.astype(F32)*ob.astype(F32))
            delta=jnp.sum(prod.T,axis=0,keepdims=True)
            s_s[0:npre]=dot(v_s[0:npre],dob,NT)
            s_s[npre:]=dot(v_s[pl.ds(w0,win)],dob,NT)
            for j in range(nk//ch):
                d=w_s[j*ch:(j+1)*ch].astype(F32)*(s_s[j*ch:(j+1)*ch]-delta)
                ds_s[j*ch:(j+1)*ch]=d.astype(BF)
            gqt=(dot(kt_s[:,0:npre],ds_s[0:npre])+dot(kt_s[:,pl.ds(w0,win)],ds_s[npre:]))*scale
            gq=gqt.T.astype(BF)
            gq_ref[pl.ds(r0,rb),pl.ds(c0,2*dh)]=jnp.concatenate([gq[:rb],gq[rb:]],axis=1)
            gk_s[0:npre]+=dot(ds_s[0:npre],q)
            gk_s[pl.ds(w0,win)]+=dot(ds_s[npre:],q)
            gv_s[0:npre]+=dot(w_s[0:npre],dob)
            gv_s[pl.ds(w0,win)]+=dot(w_s[npre:],dob)
            return 0
        lax.fori_loop(0,heads//2,pair,0)
        return 0
    lax.fori_loop(0,rows//rb,block,0)
    gp_ref[:,0:dh]=gk_s[0:npre]*scale
    gp_ref[:,dh:]=gv_s[0:npre]
    gw_ref[:,0:dh]=gk_s[npre:]*scale
    gw_ref[:,dh:]=gv_s[npre:]

def attend(q,up,kvp,kvprev,kvown,lengths,shard):
    rows=q.shape[0]; npre=kvp.shape[0]; dh=128; rb=128; win=rows+rb; nk=npre+win; tot=npre+2*rows
    vm=pl.BlockSpec(memory_space=pltpu.VMEM); sm=pl.BlockSpec(memory_space=pltpu.SMEM)
    sds=jax.ShapeDtypeStruct
    return pl.pallas_call(kernel,
      in_specs=[sm,sm]+[vm]*5, out_specs=[vm]*4,
      out_shape=[sds(q.shape,BF),sds(q.shape,BF),sds((npre,2*dh),F32),sds((2*rows,2*dh),F32)],
      scratch_shapes=[pltpu.VMEM((tot,dh),BF),pltpu.VMEM((tot,dh),BF),pltpu.VMEM((dh,tot),BF),pltpu.VMEM((dh,tot),BF),
         pltpu.VMEM((win,rb),F32),pltpu.VMEM((nk,2*rb),F32),pltpu.VMEM((nk,2*rb),BF),pltpu.VMEM((nk,2*rb),BF),
         pltpu.VMEM((tot,dh),F32),pltpu.VMEM((tot,dh),F32)],
      compiler_params=pltpu.CompilerParams(vmem_limit_bytes=56*2**20),
      name="attend")(lengths,shard,q,up,kvp,kvprev,kvown)


def ring(block, distance):
    size = lax.axis_size("seq")
    return lax.ppermute(block, "seq", [(i, (i + distance) % size) for i in range(size)])


def body(queries, resp_kv, prefix_kv, lengths, upstream):
    rows = queries.shape[1]
    dh = resp_kv.shape[2] // 2
    n_seq = lax.axis_size("seq")
    n_prompt = lax.axis_size("prompt")
    shard = lax.axis_index("seq").astype(jnp.int32)
    part = prefix_kv.shape[1]
    prev = ring(resp_kv[0], 1)
    count = jnp.broadcast_to(jnp.sum(lengths[0]), (8, 128))
    route = [(p * n_seq + s, (p ^ s) * n_seq + s) for p in range(n_prompt) for s in range(n_seq)]
    count = lax.ppermute(count, ("prompt", "seq"), route)
    spread = jnp.broadcast_to(prefix_kv, (n_seq, part, 2 * dh))
    prefix_all = lax.all_to_all(spread, "seq", split_axis=0, concat_axis=0, tiled=True)
    prefix_all = prefix_all.reshape(n_seq * part, 2 * dh)
    attended, grad_query, gp, gw = attend(
        queries[0], upstream[0], prefix_all, prev, resp_kv[0], lengths, shard[None]
    )
    returned = ring(gw[:rows].astype(BF), -1)
    high = (count[0, 0] // 128).astype(BF)
    low = (count[0, 0] % 128).astype(BF)
    tail = jnp.concatenate(
        [jnp.full((n_seq, 16, dh), high, BF), jnp.full((n_seq, 16, dh), low, BF)], axis=2
    )
    packet = jnp.concatenate([gp.astype(BF).reshape(n_seq, part, 2 * dh), tail], axis=1)
    packet = lax.all_to_all(packet, "seq", split_axis=0, concat_axis=0, tiled=True).astype(F32)
    total = jnp.sum(packet[:, part, 0] * 128.0 + packet[:, part, dh])
    factor = jnp.float32(n_prompt * n_seq * rows) / total
    grad_prefix = jnp.sum(packet[:, :part], axis=0) * factor
    grad_resp = (gw[rows:] + returned.astype(F32)) * factor
    grad_query = (grad_query.astype(F32) * factor).astype(BF)
    return (attended[None], grad_query[None], grad_resp[None], grad_prefix[None])


def solution(mesh):
    spec = P("prompt", "seq", None)
    return jax.shard_map(
        body,
        mesh=mesh,
        in_specs=(spec, spec, spec, P("prompt", None), spec),
        out_specs=(spec, spec, spec, spec),
        check_vma=False,
    )
```

```python
import functools
import math

import jax
import jax.numpy as jnp
from jax import lax
from jax.experimental import pallas as pl
from jax.experimental.pallas import tpu as pltpu
from jax.sharding import PartitionSpec as P

F32 = jnp.float32
BF = jnp.bfloat16
NN = (((1,), (0,)), ((), ()))
NT = (((1,), (1,)), ((), ()))
DH = 128
RB = 128
CH = 64
BLOCK = 1408
SCALE = DH**-0.5
LOG2_SCALE = SCALE * math.log2(math.e)


def dot(a, b, dims=NN):
    return lax.dot_general(a, b, dims, preferred_element_type=F32)


def tile(p):
    return slice(p * 2 * RB, (p + 1) * 2 * RB)


def stack_heads(pair):
    return jnp.concatenate([pair[:, :DH], pair[:, DH:]], axis=0)


def unstack_heads(rows):
    return jnp.concatenate([rows[:RB], rows[RB:]], axis=1)


def first_slots(len_ref, first, width):
    pos = first + lax.broadcasted_iota(jnp.int32, (1, width), 1)
    start = jnp.zeros((1, width), jnp.int32)
    end = jnp.int32(0)
    for r in range(len_ref.shape[1]):
        end = end + len_ref[0, r]
        start = jnp.where(pos >= end, end, start)
    return pos, start, pos < end


def row_total(values):
    return jnp.sum(values.reshape(values.shape[0] // 8, 8, values.shape[1]), axis=0)


def row_peak(values):
    return jnp.max(values.reshape(values.shape[0] // 8, 8, values.shape[1]), axis=0)


def interleave(*streams):
    pieces = [list(stream) for stream in streams]
    longest = max(len(items) for items in pieces)
    for i in range(longest):
        for items in pieces:
            for piece in items[i * len(items) // longest : (i + 1) * len(items) // longest]:
                piece()


def attend(len_ref, shard_ref, q_ref, up_ref, kv_ref, prev_ref, own_ref,
           o_ref, gq_ref, packet_ref, gprev_ref, gown_ref,
           k_s, v_s, kt_s, vt_s, bias_s, s_s, t_s, w_s, ds_s, q_s, d_s, gk_s, gv_s):
    rows = prev_ref.shape[0]
    prefix = kv_ref.shape[0]
    win = rows + RB
    n = prefix + win
    tiles = q_ref.shape[1] // (2 * DH)
    step = pl.program_id(0)

    @pl.when(step == 0)
    def _():
        for ref, low in ((kv_ref, 0), (prev_ref, prefix), (own_ref, prefix + rows)):
            high = low + ref.shape[0]
            k_s[low:high] = ref[:, :DH]
            v_s[low:high] = ref[:, DH:]
            kt_s[:, low:high] = ref[:, :DH].T
            vt_s[:, low:high] = ref[:, DH:].T
        gk_s[...] = jnp.zeros_like(gk_s)
        gv_s[...] = jnp.zeros_like(gv_s)

    first = shard_ref[0] * rows + step * RB
    pos, start, live = first_slots(len_ref, first, RB)
    live = jnp.concatenate([live, live], axis=1)
    slot = first - rows + lax.broadcasted_iota(jnp.int32, (win, RB), 0)
    bias_s[...] = jnp.where((slot >= start) & (slot <= pos), 0.0, -jnp.inf).astype(F32)
    span = pl.ds(pl.multiple_of(prefix + step * RB, RB), win)
    peak, part, inv, delta = {}, {}, {}, {}

    def key_blocks(size):
        for j in range(0, prefix, size):
            block = slice(j, min(j + size, prefix))
            yield block, block
        for j in range(0, win, size):
            high = min(j + size, win)
            whole = pl.ds(pl.multiple_of(prefix + step * RB + j, RB), high - j)
            yield slice(prefix + j, prefix + high), whole

    def scores(p):
        def piece(here, there):
            s_s[here, tile(p)] = dot(k_s[there], q_s[tile(p)], NT)

        def stack():
            q_s[tile(p)] = stack_heads(q_ref[:, tile(p)])

        return [stack] + [functools.partial(piece, *block) for block in key_blocks(BLOCK)]

    def peaks(p):
        def piece(j):
            s = s_s[j : j + CH, tile(p)] * LOG2_SCALE
            if j >= prefix:
                b = bias_s[j - prefix : j - prefix + CH]
                s = s + jnp.concatenate([b, b], axis=1)
            s_s[j : j + CH, tile(p)] = s
            top = row_peak(s)
            peak[p] = jnp.maximum(peak[p], top) if j else top

        def final():
            peak[p] = jnp.max(peak[p], axis=0, keepdims=True)

        return [functools.partial(piece, j) for j in range(0, n, CH)] + [final]

    def weigh(p):
        def piece(j):
            w = jnp.exp2(s_s[j : j + CH, tile(p)] - peak[p])
            part[p] = part[p] + row_total(w) if j else row_total(w)
            w_s[j : j + CH, tile(p)] = w.astype(BF)

        def final():
            inv[p] = jnp.where(live, 1.0 / jnp.sum(part[p], axis=0, keepdims=True), 0.0)
            spread = jnp.broadcast_to(inv[p], (DH, 2 * RB)).T
            d_s[tile(p)] = (stack_heads(up_ref[:, tile(p)]).astype(F32) * spread).astype(BF)

        return [functools.partial(piece, j) for j in range(0, n, CH)] + [final]

    def mix(p):
        def piece():
            ot = dot(vt_s[:, :prefix], w_s[:prefix, tile(p)]) + dot(vt_s[:, span], w_s[prefix:, tile(p)])
            o = (ot * inv[p]).T.astype(BF)
            o_ref[:, tile(p)] = unstack_heads(o)
            product = d_s[tile(p)].astype(F32) * o.astype(F32)
            delta[p] = jnp.sum(product.T, axis=0, keepdims=True)

        return [piece]

    def slopes(p):
        def piece(here, there):
            t_s[here, tile(p)] = dot(v_s[there], d_s[tile(p)], NT)

        return [functools.partial(piece, *block) for block in key_blocks(BLOCK)]

    def score_grads(p):
        def piece(j):
            w = w_s[j : j + CH, tile(p)].astype(F32)
            ds_s[j : j + CH, tile(p)] = (w * (t_s[j : j + CH, tile(p)] - delta[p])).astype(BF)

        return [functools.partial(piece, j) for j in range(0, n, CH)]

    def key_sums(total_s, left_s, right_s):
        def piece(here, there):
            total_s[there] += dot(left_s[here], right_s[...])

        return [functools.partial(piece, *block) for block in key_blocks(BLOCK)]

    def query_grads(p):
        def piece():
            gqt = dot(kt_s[:, :prefix], ds_s[:prefix, tile(p)]) + dot(kt_s[:, span], ds_s[prefix:, tile(p)])
            gq_ref[:, tile(p)] = unstack_heads((gqt * SCALE).T.astype(BF))

        return [piece]

    for stage in (scores, peaks, weigh, mix, slopes, score_grads):
        for p in range(tiles):
            interleave(stage(p))
    interleave(key_sums(gv_s, w_s, d_s))
    for p in range(tiles):
        interleave(query_grads(p))
    interleave(key_sums(gk_s, ds_s, q_s))

    @pl.when(step == pl.num_programs(0) - 1)
    def _():
        gprev_ref[:, :DH] = (gk_s[prefix : prefix + rows] * SCALE).astype(BF)
        gprev_ref[:, DH:] = gv_s[prefix : prefix + rows].astype(BF)
        gown_ref[:, :DH] = gk_s[prefix + rows :] * SCALE
        gown_ref[:, DH:] = gv_s[prefix + rows :]
        parts, each, _ = packet_ref.shape
        for i in range(parts):
            own = slice(i * each, (i + 1) * each)
            packet_ref[i, :, :DH] = (gk_s[own] * SCALE).astype(BF)
            packet_ref[i, :, DH:] = gv_s[own].astype(BF)


def call(kernel, name, steps, in_specs, outs, scratch, flops, traffic):
    return pl.pallas_call(
        kernel,
        name=name,
        grid=(steps,),
        in_specs=in_specs,
        out_specs=[spec for spec, _ in outs],
        out_shape=[shape for _, shape in outs],
        scratch_shapes=[pltpu.VMEM(shape, dtype) for shape, dtype in scratch],
        compiler_params=pltpu.CompilerParams(
            dimension_semantics=("arbitrary",), vmem_limit_bytes=56 * 2**20
        ),
        cost_estimate=pl.CostEstimate(flops=flops, bytes_accessed=traffic, transcendentals=0),
    )


def kernels(rows, prefix, heads, parts):
    steps = rows // RB
    cols = heads * RB
    win = rows + RB
    small = pl.BlockSpec(memory_space=pltpu.SMEM)
    row_spec = pl.BlockSpec((RB, heads * DH), lambda i: (i, 0))
    whole = lambda *shape: pl.BlockSpec(shape, lambda i: (0,) * len(shape))
    kv_spec = whole(rows, 2 * DH)
    sds = jax.ShapeDtypeStruct
    row_out = (row_spec, sds((rows, heads * DH), BF))
    packet = (parts, prefix // parts, 2 * DH)
    n = prefix + win
    every = prefix + 2 * rows
    return call(
        attend, "attend", steps,
        [small, small, row_spec, row_spec, whole(prefix, 2 * DH), kv_spec, kv_spec],
        [row_out, row_out, (whole(*packet), sds(packet, BF)),
         (kv_spec, sds((rows, 2 * DH), BF)), (kv_spec, sds((rows, 2 * DH), F32))],
        [((every, DH), BF), ((every, DH), BF), ((DH, every), BF), ((DH, every), BF), ((win, RB), F32),
         ((n, cols), F32), ((n, cols), F32), ((n, cols), BF), ((n, cols), BF),
         ((cols, DH), BF), ((cols, DH), BF), ((every, DH), F32), ((every, DH), F32)],
        12 * rows * heads * DH * n, 6 * 2**20,
    )


def ring(block, distance):
    size = lax.axis_size("seq")
    return lax.ppermute(block, "seq", [(i, (i + distance) % size) for i in range(size)])


def exchange(packets):
    return lax.all_to_all(packets, "seq", split_axis=0, concat_axis=0, tiled=True)


def pair_routes(n_prompt):
    side = math.isqrt(n_prompt)

    def paired(k, odd):
        return ((k + odd) ^ 1) - odd

    for odd in (0, 1):
        yield [(p, (paired(p // side, odd) % side) * side + p % side) for p in range(n_prompt)]
    for odd in (0, 1):
        yield [(p, p // side * side + paired(p % side, odd) % side) for p in range(n_prompt)]


def body(queries, resp_kv, prefix_kv, lengths, upstream):
    rows, width = queries.shape[1:]
    n_seq = lax.axis_size("seq")
    n_prompt = lax.axis_size("prompt")
    shard = lax.axis_index("seq").astype(jnp.int32)[None]
    part = prefix_kv.shape[1]
    core = kernels(rows, n_seq * part, width // DH, n_seq)
    first, second, third, fourth = pair_routes(n_prompt)
    counts = lengths
    counts = counts + lax.ppermute(counts, "prompt", first)
    prev = ring(resp_kv[0], 1)
    prefix_all = exchange(jnp.broadcast_to(prefix_kv, (n_seq, part, 2 * DH)))
    prefix_all = prefix_all.reshape(n_seq * part, 2 * DH)
    counts = counts + lax.ppermute(counts, "prompt", second)
    incoming = lax.ppermute(counts, "prompt", third)
    attended, grad_query, packet, g_prev, g_own = core(
        lengths, shard, queries[0], upstream[0], prefix_all, prev, resp_kv[0]
    )
    packet, incoming = lax.optimization_barrier((packet, incoming))
    packet = exchange(packet)
    returned = ring(g_prev, -1)
    counts = counts + incoming
    counts = counts + lax.ppermute(counts, "prompt", fourth)
    factor = jnp.float32(n_prompt * n_seq * rows) / jnp.sum(counts).astype(F32)
    grad_query = (grad_query.astype(F32) * factor).astype(BF)
    grad_prefix = jnp.sum(packet.astype(F32), axis=0) * factor
    grad_resp = (g_own + returned.astype(F32)) * factor
    return (attended[None], grad_query[None], grad_resp[None], grad_prefix[None])


def solution(mesh):
    spec = P("prompt", "seq", None)
    return jax.shard_map(
        body,
        mesh=mesh,
        in_specs=(spec, spec, spec, P("prompt", None), spec),
        out_specs=(spec, spec, spec, spec),
        check_vma=False,
    )
```

```python
import functools
import math

import jax
import jax.numpy as jnp
from jax import lax
from jax.experimental import pallas as pl
from jax.experimental.pallas import tpu as pltpu
from jax.sharding import PartitionSpec as P

F32 = jnp.float32
BF = jnp.bfloat16
NN = (((1,), (0,)), ((), ()))
NT = (((1,), (1,)), ((), ()))
DH = 128
RB = 128
CH = 64
BLOCK = 1408
SCALE = DH**-0.5
LOG2_SCALE = SCALE * math.log2(math.e)


def dot(a, b, dims=NN):
    return lax.dot_general(a, b, dims, preferred_element_type=F32)


def tile(p):
    return slice(p * 2 * RB, (p + 1) * 2 * RB)


def stack_heads(pair):
    return jnp.concatenate([pair[:, :DH], pair[:, DH:]], axis=0)


def unstack_heads(rows):
    return jnp.concatenate([rows[:RB], rows[RB:]], axis=1)


def first_slots(len_ref, first, width):
    pos = first + lax.broadcasted_iota(jnp.int32, (1, width), 1)
    start = jnp.zeros((1, width), jnp.int32)
    end = jnp.int32(0)
    for r in range(len_ref.shape[1]):
        end = end + len_ref[0, r]
        start = jnp.where(pos >= end, end, start)
    return pos, start, pos < end


def row_total(values):
    return jnp.sum(values.reshape(values.shape[0] // 8, 8, values.shape[1]), axis=0)


def row_peak(values):
    return jnp.max(values.reshape(values.shape[0] // 8, 8, values.shape[1]), axis=0)


def interleave(*streams):
    pieces = [list(stream) for stream in streams]
    longest = max(len(items) for items in pieces)
    for i in range(longest):
        for items in pieces:
            for piece in items[i * len(items) // longest : (i + 1) * len(items) // longest]:
                piece()


def attend(len_ref, shard_ref, q_ref, up_ref, kv_ref, prev_ref, own_ref,
           o_ref, gq_ref, packet_ref, gprev_ref, gown_ref,
           k_s, v_s, kt_s, vt_s, bias_s, s_s, t_s, w_s, ds_s, q_s, d_s, gk_s, gv_s):
    rows = prev_ref.shape[0]
    prefix = kv_ref.shape[0]
    win = rows + RB
    n = prefix + win
    tiles = q_ref.shape[1] // (2 * DH)
    step = pl.program_id(0)

    @pl.when(step == 0)
    def _():
        for ref, low in ((kv_ref, 0), (prev_ref, prefix), (own_ref, prefix + rows)):
            high = low + ref.shape[0]
            k_s[low:high] = ref[:, :DH]
            v_s[low:high] = ref[:, DH:]
            kt_s[:, low:high] = ref[:, :DH].T
            vt_s[:, low:high] = ref[:, DH:].T
        gk_s[...] = jnp.zeros_like(gk_s)
        gv_s[...] = jnp.zeros_like(gv_s)

    first = shard_ref[0] * rows + step * RB
    pos, start, live = first_slots(len_ref, first, RB)
    live = jnp.concatenate([live, live], axis=1)
    slot = first - rows + lax.broadcasted_iota(jnp.int32, (win, RB), 0)
    bias_s[...] = jnp.where((slot >= start) & (slot <= pos), 0.0, -jnp.inf).astype(F32)
    span = pl.ds(pl.multiple_of(prefix + step * RB, RB), win)
    peak, part, inv, delta = {}, {}, {}, {}

    def key_blocks(size):
        for j in range(0, prefix, size):
            block = slice(j, min(j + size, prefix))
            yield block, block
        for j in range(0, win, size):
            high = min(j + size, win)
            whole = pl.ds(pl.multiple_of(prefix + step * RB + j, RB), high - j)
            yield slice(prefix + j, prefix + high), whole

    def scores(p):
        def piece(here, there):
            s_s[here, tile(p)] = dot(k_s[there], q_s[tile(p)], NT)

        def stack():
            q_s[tile(p)] = stack_heads(q_ref[:, tile(p)])

        return [stack] + [functools.partial(piece, *block) for block in key_blocks(BLOCK)]

    def peaks(p):
        def piece(j):
            s = s_s[j : j + CH, tile(p)] * LOG2_SCALE
            if j >= prefix:
                b = bias_s[j - prefix : j - prefix + CH]
                s = s + jnp.concatenate([b, b], axis=1)
            s_s[j : j + CH, tile(p)] = s
            top = row_peak(s)
            peak[p] = jnp.maximum(peak[p], top) if j else top

        def final():
            peak[p] = jnp.max(peak[p], axis=0, keepdims=True)

        return [functools.partial(piece, j) for j in range(0, n, CH)] + [final]

    def weigh(p):
        def piece(j):
            w = jnp.exp2(s_s[j : j + CH, tile(p)] - peak[p])
            part[p] = part[p] + row_total(w) if j else row_total(w)
            w_s[j : j + CH, tile(p)] = w.astype(BF)

        def final():
            inv[p] = jnp.where(live, 1.0 / jnp.sum(part[p], axis=0, keepdims=True), 0.0)
            spread = jnp.broadcast_to(inv[p], (DH, 2 * RB)).T
            d_s[tile(p)] = (stack_heads(up_ref[:, tile(p)]).astype(F32) * spread).astype(BF)

        return [functools.partial(piece, j) for j in range(0, n, CH)] + [final]

    def mix(p):
        def piece():
            ot = dot(vt_s[:, :prefix], w_s[:prefix, tile(p)]) + dot(vt_s[:, span], w_s[prefix:, tile(p)])
            o = (ot * inv[p]).T.astype(BF)
            o_ref[:, tile(p)] = unstack_heads(o)
            product = d_s[tile(p)].astype(F32) * o.astype(F32)
            delta[p] = jnp.sum(product.T, axis=0, keepdims=True)

        return [piece]

    def slopes(p):
        def piece(here, there):
            t_s[here, tile(p)] = dot(v_s[there], d_s[tile(p)], NT)

        return [functools.partial(piece, *block) for block in key_blocks(BLOCK)]

    def score_grads(p):
        def piece(j):
            w = w_s[j : j + CH, tile(p)].astype(F32)
            ds_s[j : j + CH, tile(p)] = (w * (t_s[j : j + CH, tile(p)] - delta[p])).astype(BF)

        return [functools.partial(piece, j) for j in range(0, n, CH)]

    def key_sums(total_s, left_s, right_s):
        def piece(here, there):
            total_s[there] += dot(left_s[here], right_s[...])

        return [functools.partial(piece, *block) for block in key_blocks(BLOCK)]

    def query_grads(p):
        def piece():
            gqt = dot(kt_s[:, :prefix], ds_s[:prefix, tile(p)]) + dot(kt_s[:, span], ds_s[prefix:, tile(p)])
            gq_ref[:, tile(p)] = unstack_heads((gqt * SCALE).T.astype(BF))

        return [piece]

    for stage in (scores, peaks, weigh, mix, slopes, score_grads):
        for p in range(tiles):
            interleave(stage(p))
    interleave(key_sums(gv_s, w_s, d_s))
    for p in range(tiles):
        interleave(query_grads(p))
    interleave(key_sums(gk_s, ds_s, q_s))

    @pl.when(step == pl.num_programs(0) - 1)
    def _():
        gprev_ref[:, :DH] = (gk_s[prefix : prefix + rows] * SCALE).astype(BF)
        gprev_ref[:, DH:] = gv_s[prefix : prefix + rows].astype(BF)
        gown_ref[:, :DH] = gk_s[prefix + rows :] * SCALE
        gown_ref[:, DH:] = gv_s[prefix + rows :]
        parts, each, _ = packet_ref.shape
        for i in range(parts):
            own = slice(i * each, (i + 1) * each)
            packet_ref[i, :, :DH] = (gk_s[own] * SCALE).astype(BF)
            packet_ref[i, :, DH:] = gv_s[own].astype(BF)


def call(kernel, name, steps, in_specs, outs, scratch, flops, traffic):
    return pl.pallas_call(
        kernel,
        name=name,
        grid=(steps,),
        in_specs=in_specs,
        out_specs=[spec for spec, _ in outs],
        out_shape=[shape for _, shape in outs],
        scratch_shapes=[pltpu.VMEM(shape, dtype) for shape, dtype in scratch],
        compiler_params=pltpu.CompilerParams(
            dimension_semantics=("arbitrary",), vmem_limit_bytes=50 * 2**20
        ),
        cost_estimate=pl.CostEstimate(flops=flops, bytes_accessed=traffic, transcendentals=0),
    )


def kernels(rows, prefix, heads, parts):
    steps = rows // RB
    cols = heads * RB
    win = rows + RB
    small = pl.BlockSpec(memory_space=pltpu.SMEM)
    row_spec = pl.BlockSpec((RB, heads * DH), lambda i: (i, 0))
    whole = lambda *shape: pl.BlockSpec(shape, lambda i: (0,) * len(shape))
    kv_spec = whole(rows, 2 * DH)
    sds = jax.ShapeDtypeStruct
    row_out = (row_spec, sds((rows, heads * DH), BF))
    packet = (parts, prefix // parts, 2 * DH)
    n = prefix + win
    every = prefix + 2 * rows
    return call(
        attend, "attend", steps,
        [small, small, row_spec, row_spec, whole(prefix, 2 * DH), kv_spec, kv_spec],
        [row_out, row_out, (whole(*packet), sds(packet, BF)),
         (kv_spec, sds((rows, 2 * DH), BF)), (kv_spec, sds((rows, 2 * DH), F32))],
        [((every, DH), BF), ((every, DH), BF), ((DH, every), BF), ((DH, every), BF), ((win, RB), F32),
         ((n, cols), F32), ((n, cols), F32), ((n, cols), BF), ((n, cols), BF),
         ((cols, DH), BF), ((cols, DH), BF), ((every, DH), F32), ((every, DH), F32)],
        12 * rows * heads * DH * n, 6 * 2**20,
    )


def ring(block, distance):
    size = lax.axis_size("seq")
    return lax.ppermute(block, "seq", [(i, (i + distance) % size) for i in range(size)])


def exchange(packets):
    return lax.all_to_all(packets, "seq", split_axis=0, concat_axis=0, tiled=True)


def pair_routes(n_prompt):
    side = math.isqrt(n_prompt)

    def paired(k, odd):
        return ((k + odd) ^ 1) - odd

    for odd in (0, 1):
        yield [(p, (paired(p // side, odd) % side) * side + p % side) for p in range(n_prompt)]
    for odd in (0, 1):
        yield [(p, p // side * side + paired(p % side, odd) % side) for p in range(n_prompt)]


def body(queries, resp_kv, prefix_kv, lengths, upstream):
    rows, width = queries.shape[1:]
    n_seq = lax.axis_size("seq")
    n_prompt = lax.axis_size("prompt")
    shard = lax.axis_index("seq").astype(jnp.int32)[None]
    part = prefix_kv.shape[1]
    core = kernels(rows, n_seq * part, width // DH, n_seq)
    first, second, third, fourth = pair_routes(n_prompt)
    counts = lengths
    counts = counts + lax.ppermute(counts, "prompt", first)
    prev = ring(resp_kv[0], 1)
    prefix_all = exchange(jnp.broadcast_to(prefix_kv, (n_seq, part, 2 * DH)))
    prefix_all = prefix_all.reshape(n_seq * part, 2 * DH)
    counts = counts + lax.ppermute(counts, "prompt", second)
    incoming = lax.ppermute(counts, "prompt", third)
    attended, grad_query, packet, g_prev, g_own = core(
        lengths, shard, queries[0], upstream[0], prefix_all, prev, resp_kv[0]
    )
    packet, incoming = lax.optimization_barrier((packet, incoming))
    packet = exchange(packet)
    returned = ring(g_prev, -1)
    counts = counts + incoming
    counts = counts + lax.ppermute(counts, "prompt", fourth)
    factor = jnp.float32(n_prompt * n_seq * rows) / jnp.sum(counts).astype(F32)
    grad_query = (grad_query.astype(F32) * factor).astype(BF)
    grad_prefix = jnp.sum(packet.astype(F32), axis=0) * factor
    grad_resp = (g_own + returned.astype(F32)) * factor
    return (attended[None], grad_query[None], grad_resp[None], grad_prefix[None])


def solution(mesh):
    spec = P("prompt", "seq", None)
    return jax.shard_map(
        body,
        mesh=mesh,
        in_specs=(spec, spec, spec, P("prompt", None), spec),
        out_specs=(spec, spec, spec, spec),
        check_vma=False,
    )
```

```python
import functools
import math

import jax
import jax.numpy as jnp
from jax import lax
from jax.experimental import pallas as pl
from jax.experimental.pallas import tpu as pltpu
from jax.sharding import PartitionSpec as P

F32 = jnp.float32
BF = jnp.bfloat16
NN = (((1,), (0,)), ((), ()))
NT = (((1,), (1,)), ((), ()))
DH = 128
RB = 128
CH = 64
BLOCK = 1408
SCALE = DH**-0.5
LOG2_SCALE = SCALE * math.log2(math.e)


def dot(a, b, dims=NN):
    return lax.dot_general(a, b, dims, preferred_element_type=F32)


def tile(p):
    return slice(p * 2 * RB, (p + 1) * 2 * RB)


def stack_heads(pair):
    return jnp.concatenate([pair[:, :DH], pair[:, DH:]], axis=0)


def unstack_heads(rows):
    return jnp.concatenate([rows[:RB], rows[RB:]], axis=1)


def first_slots(len_ref, first, width):
    pos = first + lax.broadcasted_iota(jnp.int32, (1, width), 1)
    start = jnp.zeros((1, width), jnp.int32)
    end = jnp.int32(0)
    for r in range(len_ref.shape[1]):
        end = end + len_ref[0, r]
        start = jnp.where(pos >= end, end, start)
    return pos, start, pos < end


def row_total(values):
    return jnp.sum(values.reshape(values.shape[0] // 8, 8, values.shape[1]), axis=0)


def row_peak(values):
    return jnp.max(values.reshape(values.shape[0] // 8, 8, values.shape[1]), axis=0)


def interleave(*streams):
    pieces = [list(stream) for stream in streams]
    longest = max(len(items) for items in pieces)
    for i in range(longest):
        for items in pieces:
            for piece in items[i * len(items) // longest : (i + 1) * len(items) // longest]:
                piece()


def attend(len_ref, shard_ref, q_ref, up_ref, kv_ref, prev_ref, own_ref,
           o_ref, gq_ref, packet_ref, gprev_ref, gown_ref,
           k_s, v_s, kt_s, vt_s, bias_s, s_s, t_s, w_s, ds_s, q_s, d_s, gk_s, gv_s):
    rows = prev_ref.shape[0]
    prefix = kv_ref.shape[0]
    win = rows + RB
    n = prefix + win
    tiles = q_ref.shape[1] // (2 * DH)
    step = pl.program_id(0)

    @pl.when(step == 0)
    def _():
        for ref, low in ((kv_ref, 0), (prev_ref, prefix), (own_ref, prefix + rows)):
            high = low + ref.shape[0]
            k_s[low:high] = ref[:, :DH]
            v_s[low:high] = ref[:, DH:]
            kt_s[:, low:high] = ref[:, :DH].T
            vt_s[:, low:high] = ref[:, DH:].T
        gk_s[...] = jnp.zeros_like(gk_s)
        gv_s[...] = jnp.zeros_like(gv_s)

    first = shard_ref[0] * rows + step * RB
    pos, start, live = first_slots(len_ref, first, RB)
    live = jnp.concatenate([live, live], axis=1)
    slot = first - rows + lax.broadcasted_iota(jnp.int32, (win, RB), 0)
    bias_s[...] = jnp.where((slot >= start) & (slot <= pos), 0.0, -jnp.inf).astype(F32)
    span = pl.ds(pl.multiple_of(prefix + step * RB, RB), win)
    peak, part, inv, delta = {}, {}, {}, {}

    def key_blocks(size):
        for j in range(0, prefix, size):
            block = slice(j, min(j + size, prefix))
            yield block, block
        for j in range(0, win, size):
            high = min(j + size, win)
            whole = pl.ds(pl.multiple_of(prefix + step * RB + j, RB), high - j)
            yield slice(prefix + j, prefix + high), whole

    def scores(p):
        def piece(here, there):
            s_s[here, tile(p)] = dot(k_s[there], q_s[tile(p)], NT)

        def stack():
            q_s[tile(p)] = stack_heads(q_ref[:, tile(p)])

        return [stack] + [functools.partial(piece, *block) for block in key_blocks(BLOCK)]

    def peaks(p):
        def piece(j):
            s = s_s[j : j + CH, tile(p)] * LOG2_SCALE
            if j >= prefix:
                b = bias_s[j - prefix : j - prefix + CH]
                s = s + jnp.concatenate([b, b], axis=1)
            s_s[j : j + CH, tile(p)] = s
            top = row_peak(s)
            peak[p] = jnp.maximum(peak[p], top) if j else top

        def final():
            peak[p] = jnp.max(peak[p], axis=0, keepdims=True)

        return [functools.partial(piece, j) for j in range(0, n, CH)] + [final]

    def weigh(p):
        def piece(j):
            w = jnp.exp2(s_s[j : j + CH, tile(p)] - peak[p])
            part[p] = part[p] + row_total(w) if j else row_total(w)
            w_s[j : j + CH, tile(p)] = w.astype(BF)

        def final():
            inv[p] = jnp.where(live, 1.0 / jnp.sum(part[p], axis=0, keepdims=True), 0.0)
            spread = jnp.broadcast_to(inv[p], (DH, 2 * RB)).T
            d_s[tile(p)] = (stack_heads(up_ref[:, tile(p)]).astype(F32) * spread).astype(BF)

        return [functools.partial(piece, j) for j in range(0, n, CH)] + [final]

    def mix(p):
        def piece():
            ot = dot(vt_s[:, :prefix], w_s[:prefix, tile(p)]) + dot(vt_s[:, span], w_s[prefix:, tile(p)])
            o = (ot * inv[p]).T.astype(BF)
            o_ref[:, tile(p)] = unstack_heads(o)
            product = d_s[tile(p)].astype(F32) * o.astype(F32)
            delta[p] = jnp.sum(product.T, axis=0, keepdims=True)

        return [piece]

    def slopes(p):
        def piece(here, there):
            t_s[here, tile(p)] = dot(v_s[there], d_s[tile(p)], NT)

        return [functools.partial(piece, *block) for block in key_blocks(BLOCK)]

    def score_grads(p):
        def piece(j):
            w = w_s[j : j + CH, tile(p)].astype(F32)
            ds_s[j : j + CH, tile(p)] = (w * (t_s[j : j + CH, tile(p)] - delta[p])).astype(BF)

        return [functools.partial(piece, j) for j in range(0, n, CH)]

    def key_sums(total_s, left_s, right_s):
        def piece(here, there):
            total_s[there] += dot(left_s[here], right_s[...])

        return [functools.partial(piece, *block) for block in key_blocks(BLOCK)]

    def query_grads(p):
        def piece():
            gqt = dot(kt_s[:, :prefix], ds_s[:prefix, tile(p)]) + dot(kt_s[:, span], ds_s[prefix:, tile(p)])
            gq_ref[:, tile(p)] = unstack_heads((gqt * SCALE).T.astype(BF))

        return [piece]

    for stage in (scores, peaks, weigh, mix, slopes, score_grads):
        for p in range(tiles):
            interleave(stage(p))
    interleave(key_sums(gv_s, w_s, d_s))
    for p in range(tiles):
        interleave(query_grads(p))
    interleave(key_sums(gk_s, ds_s, q_s))

    @pl.when(step == pl.num_programs(0) - 1)
    def _():
        gprev_ref[:, :DH] = (gk_s[prefix : prefix + rows] * SCALE).astype(BF)
        gprev_ref[:, DH:] = gv_s[prefix : prefix + rows].astype(BF)
        gown_ref[:, :DH] = gk_s[prefix + rows :] * SCALE
        gown_ref[:, DH:] = gv_s[prefix + rows :]
        parts, each, _ = packet_ref.shape
        for i in range(parts):
            own = slice(i * each, (i + 1) * each)
            packet_ref[i, :, :DH] = (gk_s[own] * SCALE).astype(BF)
            packet_ref[i, :, DH:] = gv_s[own].astype(BF)


def call(kernel, name, steps, in_specs, outs, scratch, flops, traffic):
    return pl.pallas_call(
        kernel,
        name=name,
        grid=(steps,),
        in_specs=in_specs,
        out_specs=[spec for spec, _ in outs],
        out_shape=[shape for _, shape in outs],
        scratch_shapes=[pltpu.VMEM(shape, dtype) for shape, dtype in scratch],
        compiler_params=pltpu.CompilerParams(
            dimension_semantics=("arbitrary",), vmem_limit_bytes=50 * 2**20
        ),
        cost_estimate=pl.CostEstimate(flops=flops, bytes_accessed=traffic, transcendentals=0),
    )


def kernels(rows, prefix, heads, parts):
    steps = rows // RB
    cols = heads * RB
    win = rows + RB
    small = pl.BlockSpec(memory_space=pltpu.SMEM)
    row_spec = pl.BlockSpec((RB, heads * DH), lambda i: (i, 0))
    whole = lambda *shape: pl.BlockSpec(shape, lambda i: (0,) * len(shape))
    kv_spec = whole(rows, 2 * DH)
    sds = jax.ShapeDtypeStruct
    row_out = (row_spec, sds((rows, heads * DH), BF))
    packet = (parts, prefix // parts, 2 * DH)
    n = prefix + win
    every = prefix + 2 * rows
    return call(
        attend, "attend", steps,
        [small, small, row_spec, row_spec, whole(prefix, 2 * DH), kv_spec, kv_spec],
        [row_out, row_out, (whole(*packet), sds(packet, BF)),
         (kv_spec, sds((rows, 2 * DH), BF)), (kv_spec, sds((rows, 2 * DH), F32))],
        [((every, DH), BF), ((every, DH), BF), ((DH, every), BF), ((DH, every), BF), ((win, RB), F32),
         ((n, cols), F32), ((n, cols), F32), ((n, cols), BF), ((n, cols), BF),
         ((cols, DH), BF), ((cols, DH), BF), ((every, DH), F32), ((every, DH), F32)],
        12 * rows * heads * DH * n, 6 * 2**20,
    )


def ring(block, distance):
    size = lax.axis_size("seq")
    return lax.ppermute(block, "seq", [(i, (i + distance) % size) for i in range(size)])


def exchange(packets):
    return lax.all_to_all(packets, "seq", split_axis=0, concat_axis=0, tiled=True)


def pair_routes(n_prompt):
    side = math.isqrt(n_prompt)

    def paired(k, odd):
        return ((k + odd) ^ 1) - odd

    yield [[(p, (p + turn * side) % n_prompt) for p in range(n_prompt)] for turn in range(1, side)]
    for odd in (0, 1):
        yield [(p, p // side * side + paired(p % side, odd) % side) for p in range(n_prompt)]


def body(queries, resp_kv, prefix_kv, lengths, upstream):
    rows, width = queries.shape[1:]
    n_seq = lax.axis_size("seq")
    n_prompt = lax.axis_size("prompt")
    shard = lax.axis_index("seq").astype(jnp.int32)[None]
    part = prefix_kv.shape[1]
    core = kernels(rows, n_seq * part, width // DH, n_seq)
    across, third, fourth = pair_routes(n_prompt)
    counts = lengths
    counts = counts + sum(lax.ppermute(lengths, "prompt", route) for route in across)
    prev = ring(resp_kv[0], 1)
    prefix_all = exchange(jnp.broadcast_to(prefix_kv, (n_seq, part, 2 * DH)))
    prefix_all = prefix_all.reshape(n_seq * part, 2 * DH)
    incoming = lax.ppermute(counts, "prompt", third)
    attended, grad_query, packet, g_prev, g_own = core(
        lengths, shard, queries[0], upstream[0], prefix_all, prev, resp_kv[0]
    )
    packet, incoming = lax.optimization_barrier((packet, incoming))
    packet = exchange(packet)
    returned = ring(g_prev, -1)
    counts = counts + incoming
    counts = counts + lax.ppermute(counts, "prompt", fourth)
    factor = jnp.float32(n_prompt * n_seq * rows) / jnp.sum(counts).astype(F32)
    grad_query = (grad_query.astype(F32) * factor).astype(BF)
    grad_prefix = jnp.sum(packet.astype(F32), axis=0) * factor
    grad_resp = (g_own + returned.astype(F32)) * factor
    return (attended[None], grad_query[None], grad_resp[None], grad_prefix[None])


def solution(mesh):
    spec = P("prompt", "seq", None)
    return jax.shard_map(
        body,
        mesh=mesh,
        in_specs=(spec, spec, spec, P("prompt", None), spec),
        out_specs=(spec, spec, spec, spec),
        check_vma=False,
    )
```
